32 devices in a mesh: pipe: 2 (over x), space: 16 (over z, y, core).
Axes of the slice: x: 2, y: 2, z: 4, core: 2. Of those that a mesh axis runs over, the one named last changes fastest.
Arguments:
- activations: bfloat16 [2, 2, 96, 256, 512], P('pipe', None, None, 'space'), may hold values from -6 to 6
- cotangent: bfloat16 [2, 2, 96, 256, 512], P('pipe', None, None, 'space'), may hold values from -6 to 6
- kept_modes: int32 [2, 2], P('pipe'), may hold values from 32 to 128, as said below
- weight_in: float32 [2, 2, 2, 96, 96], P('pipe'), may hold values from -0.4375 to 0.4375
- bias_in: float32 [2, 2, 2, 96], P('pipe'), may hold values from -4 to 4
- weight_out: float32 [2, 2, 2, 96, 96], P('pipe'), may hold values from -0.4375 to 0.4375
Outputs:
- grad_input: bfloat16 [2, 2, 96, 256, 512], P('pipe', None, None, 'space')
- grad_weight_in: float32 [2, 2, 2, 96, 96], P('pipe')
- grad_bias_in: float32 [2, 2, 2, 96], P('pipe')
- grad_weight_out: float32 [2, 2, 2, 96, 96], P('pipe')
- grad_bias_out: float32 [2, 2, 2, 96], P('pipe')
The draws below stay inside these ranges and needn't reach their ends.
Inputs may be any that keep to these rules, and one draw needn't show every extreme that they name: `kept_modes`: column 0 is a layer's kept longitude wavenumbers, from 64 to 128, with exactly 128 in some layer; column 1 is the kept latitude wavenumbers of each sign, from 32 to 64, with exactly 64 in some layer.
All inputs are finite; a program needn't handle non-finite values.
Results may differ from the reference program's by a relative error of at most 0.001.
Values may be sent and summed in bfloat16 or wider, within the bound.
A program may use at most 128 MiB of HBM per device.

```python
import math
import jax
import jax.numpy as jnp
from jax import lax

LAT = 256
LON = 512
KEEP_LON = 128
KEEP_LAT = 64
BLOCK = 96
BLOCKS = 2
LAYERS = 2


def draw_kept_modes(key, part):
    first = jax.random.fold_in(key, 11)
    second = jax.random.fold_in(key, 12)
    third = jax.random.fold_in(key, 13)
    fourth = jax.random.fold_in(key, 14)
    lon_count = jax.random.randint(first, (LAYERS,), KEEP_LON // 2, KEEP_LON + 1)
    lat_count = jax.random.randint(second, (LAYERS,), KEEP_LAT // 2, KEEP_LAT + 1)
    lon_count = lon_count.at[jax.random.randint(third, (), 0, LAYERS)].set(KEEP_LON)
    lat_count = lat_count.at[jax.random.randint(fourth, (), 0, LAYERS)].set(KEEP_LAT)
    return jnp.stack([lon_count, lat_count], axis=1).astype(jnp.int32)


def block_levels(rng, shape, split, least, top_value):
    gain = 1.0
    for axis_at, shards_of in split:
        heights = jax.random.uniform(jax.random.fold_in(jax.random.fold_in(rng, 6), axis_at), (shards_of,), jnp.float32, least / len(split), top_value / len(split))
        gain = gain * jnp.repeat(jnp.exp(heights), shape[axis_at] // shards_of).reshape((-1,) + (1,) * (len(shape) - 1 - axis_at))
    return gain


def gaussian(stream_key, dims, scale, reach, split=(), held_as=jnp.bfloat16):
    factor_of = block_levels(stream_key, dims, split, -0.22, 0.18) if split else 1.0
    values = jax.random.normal(stream_key, dims, jnp.float32) * scale * factor_of
    return jnp.minimum(jnp.maximum(values, -reach), reach).astype(held_as)


def setup_inputs(seed: int = 0) -> dict:
    splits = jax.random.split(jax.random.key(seed), 7)
    return {
        "activations": gaussian(splits[0], (LAYERS, BLOCKS, BLOCK, LAT, LON), 1.0, 6.0, ((0, 2), (3, 16))),
        "cotangent": gaussian(splits[1], (LAYERS, BLOCKS, BLOCK, LAT, LON), 1.0, 6.0, ((0, 2), (3, 16))),
        "kept_modes": draw_kept_modes(jax.random.fold_in(splits[6], 71), 0),
        "weight_in": gaussian(splits[3], (LAYERS, 2, BLOCKS, BLOCK, BLOCK), (2 * BLOCK) ** -0.5, 0.4375, ((0, 2),), jnp.float32),
        "bias_in": gaussian(splits[4], (LAYERS, 2, BLOCKS, BLOCK), 1.0, 4.0, ((0, 2),), jnp.float32),
        "weight_out": gaussian(splits[5], (LAYERS, 2, BLOCKS, BLOCK, BLOCK), (2 * BLOCK) ** -0.5, 0.4375, ((0, 2),), jnp.float32),
    }


HIGHEST = lax.Precision.HIGHEST

def lon_tables(length, count):
    column = jnp.arange(length, dtype=jnp.int32)
    number = jnp.arange(count, dtype=jnp.int32)
    phase = column[:, None] * number[None, :] % length
    angle = phase.astype(jnp.float32) * (2.0 * math.pi / length)
    factor = 1.0 / math.sqrt(length)
    return (jnp.cos(angle) * factor, jnp.sin(angle) * factor)

def lat_tables(length, half):
    signed = jnp.arange(2 * half, dtype=jnp.int32) - half
    row_index = jnp.arange(length, dtype=jnp.int32)
    phase = signed[:, None] * row_index[None, :] % length
    angle = phase.astype(jnp.float32) * (2.0 * math.pi / length)
    factor = 1.0 / math.sqrt(length)
    return (jnp.cos(angle) * factor, jnp.sin(angle) * factor)

def lon_forward(field, cos_table, sin_table):
    values = field.astype(jnp.float32)
    real_part = jnp.einsum('ibln,nk->iblk', values, cos_table, precision=HIGHEST)
    imag_part = -jnp.einsum('ibln,nk->iblk', values, sin_table, precision=HIGHEST)
    return jnp.stack([real_part, imag_part])

def lat_forward(spectrum, cos_table, sin_table):

    def apply(table, values):
        return jnp.einsum('fl,ibln->ibfn', table, values, precision=HIGHEST)
    real_part = apply(cos_table, spectrum[0]) + apply(sin_table, spectrum[1])
    imag_part = apply(cos_table, spectrum[1]) - apply(sin_table, spectrum[0])
    return jnp.stack([real_part, imag_part])

def lat_inverse(spectrum, cos_table, sin_table):

    def apply(table, values):
        return jnp.einsum('fl,ibfn->ibln', table, values, precision=HIGHEST)
    real_part = apply(cos_table, spectrum[0]) - apply(sin_table, spectrum[1])
    imag_part = apply(cos_table, spectrum[1]) + apply(sin_table, spectrum[0])
    return jnp.stack([real_part, imag_part])

def lon_inverse(spectrum, cos_table, sin_table):
    first = jnp.einsum('iblk,nk->ibln', spectrum[0], cos_table, precision=HIGHEST)
    second = jnp.einsum('iblk,nk->ibln', spectrum[1], sin_table, precision=HIGHEST)
    return first - second

def mode_weight(wavenumber, keep_lon, keep_lat, half):
    signed = jnp.arange(2 * half, dtype=jnp.int32) - half
    lat_kept = (signed >= -keep_lat) & (signed < keep_lat)
    lon_kept = wavenumber < keep_lon
    factor = jnp.where(wavenumber == 0, 1.0, 2.0).astype(jnp.float32)
    return (lat_kept[:, None] & lon_kept[None, :]).astype(jnp.float32) * factor[None, :]

def block_product(weights, values):
    return jnp.einsum('kij,kjm->kim', weights, values, precision=HIGHEST)

def complex_apply(weights, values):
    real_part = block_product(weights[0], values[0]) - block_product(weights[1], values[1])
    imag_part = block_product(weights[1], values[0]) + block_product(weights[0], values[1])
    return jnp.stack([real_part, imag_part])

def complex_adjoint(weights, values):
    real_t = jnp.swapaxes(weights[0], 1, 2)
    imag_t = jnp.swapaxes(weights[1], 1, 2)
    real_part = block_product(real_t, values[0]) + block_product(imag_t, values[1])
    imag_part = block_product(real_t, values[1]) - block_product(imag_t, values[0])
    return jnp.stack([real_part, imag_part])

def complex_outer(left, right):

    def outer(first, second):
        return jnp.einsum('kim,kjm->kij', first, second, precision=HIGHEST)
    real_part = outer(left[0], right[0]) + outer(left[1], right[1])
    imag_part = outer(left[1], right[0]) - outer(left[0], right[1])
    return jnp.stack([real_part, imag_part])

def gelu_pair(values):
    inner = 0.7978845608 * (values + 0.044715 * values * values * values)
    tangent = jnp.tanh(inner)
    output = 0.5 * values * (1.0 + tangent)
    slope = 0.5 * (1.0 + tangent) + 0.5 * values * (1.0 - tangent * tangent) * 0.7978845608 * (1.0 + 3.0 * 0.044715 * values * values)
    return (output, slope)

def backprop(spectrum, grad_spec, weight_in, bias_in, weight_out):
    before = complex_apply(weight_in, spectrum) + bias_in[..., None]
    hidden, slope = gelu_pair(before)
    grad_hidden = complex_adjoint(weight_out, grad_spec)
    grad_before = grad_hidden * slope
    grad_modes = complex_adjoint(weight_in, grad_before)
    grad_w_out = complex_outer(grad_spec, hidden)
    grad_w_in = complex_outer(grad_before, spectrum)
    return (grad_modes, grad_w_in, lax.optimization_barrier(jnp.sum(grad_before, axis=-1)), grad_w_out, lax.optimization_barrier(jnp.sum(grad_spec, axis=-1)))

def reference(activations, cotangent, kept_modes, weight_in, bias_in, weight_out):
    layer_count = activations.shape[0]
    nblocks = activations.shape[1]
    width = activations.shape[2]
    lon_cos, lon_sin = lon_tables(LON, KEEP_LON)
    lat_cos, lat_sin = lat_tables(LAT, KEEP_LAT)
    factor = 1.0 / math.sqrt(2 * KEEP_LAT * KEEP_LON)
    wavenumber = jnp.arange(KEEP_LON, dtype=jnp.int32)
    results = [[], [], [], [], []]
    for layer in range(layer_count):
        field = activations[layer]
        upstream = cotangent[min(layer + 1, layer_count - 1)]
        weight = mode_weight(wavenumber, kept_modes[layer, 0], kept_modes[layer, 1], KEEP_LAT)
        spectrum = lat_forward(lon_forward(field, lon_cos, lon_sin), lat_cos, lat_sin)
        grad_spec = lat_forward(lon_forward(upstream, lon_cos, lon_sin), lat_cos, lat_sin) * weight
        spectrum = spectrum.reshape(2, nblocks, width, -1)
        grad_spec = grad_spec.reshape(2, nblocks, width, -1)
        grad_modes, grad_w_in, grad_b_in, grad_w_out, grad_b_out = backprop(spectrum, grad_spec, weight_in[layer], bias_in[layer], weight_out[layer])
        grad_modes = grad_modes.reshape(2, nblocks, width, 2 * KEEP_LAT, KEEP_LON)
        back = lat_inverse(grad_modes, lat_cos, lat_sin)
        grad_field = (upstream.astype(jnp.float32) + lon_inverse(back, lon_cos, lon_sin)).astype(jnp.bfloat16)
        results[0].append(grad_field)
        results[1].append(grad_w_in * factor)
        results[2].append(grad_b_in * factor)
        results[3].append(grad_w_out * factor)
        results[4].append(grad_b_out * factor)
    return (jnp.stack(results[0]), jnp.stack(results[1]), jnp.stack(results[2]), jnp.stack(results[3]), jnp.stack(results[4]))
```

```python
import math

import jax
import jax.numpy as jnp
import numpy as np
from jax import lax
from jax.sharding import PartitionSpec as P

KEEP_LON = 128
KEEP_LAT = 64
HIGH = lax.Precision.HIGH
F32 = jnp.float32
F16 = jnp.float16


def from_behind(block, axis, distance):
    devices = range(lax.axis_size(axis))
    route = [(i - distance, i) for i in devices if i - distance in devices]
    return lax.ppermute(block, axis, route)


def lon_table(length, ndev):
    number = np.arange(KEEP_LON)[:, None] * np.arange(length)[None, :] % length
    angle = number * (2.0 * math.pi / length)
    table = np.stack([np.cos(angle), -np.sin(angle)]) / math.sqrt(length)
    table = table.reshape(2, ndev, KEEP_LON // ndev, length).transpose(1, 0, 2, 3)
    return table.astype(np.float32)


def lat_table(length):
    signed = np.arange(2 * KEEP_LAT) - KEEP_LAT
    angle = (signed[:, None] * np.arange(length)[None, :] % length) * (2.0 * math.pi / length)
    cos, sin = np.cos(angle) / math.sqrt(length), np.sin(angle) / math.sqrt(length)
    table = np.stack([np.stack([cos, sin], 1), np.stack([-sin, cos], 1)])
    return table.astype(np.float32)


def mode_mask(signed, wavenumber, keep_lon, keep_lat):
    lat_kept = (signed >= -keep_lat) & (signed < keep_lat)
    lon_kept = wavenumber < keep_lon
    factor = jnp.where(wavenumber == 0, 1.0, 2.0).astype(F32)
    return (lat_kept[:, None] & lon_kept[None, :]).astype(F32) * factor[None, :]


def real_form(weights):
    re, im = jnp.swapaxes(weights[0], 1, 2), jnp.swapaxes(weights[1], 1, 2)
    return jnp.stack([jnp.stack([re, im], 2), jnp.stack([-im, re], 2)])


def gelu_pair(values):
    inner = 0.7978845608 * (values + 0.044715 * values * values * values)
    tangent = jnp.tanh(inner)
    output = 0.5 * values * (1.0 + tangent)
    slope = 0.5 * (1.0 + tangent) + 0.5 * values * (1.0 - tangent * tangent) * 0.7978845608 * (
        1.0 + 3.0 * 0.044715 * values * values
    )
    return (output, slope)


def largest(values):
    return jnp.maximum(jnp.max(jnp.abs(values.astype(F32))), 1e-30)


def complex_outer(left, right):
    def outer(first, second):
        return jnp.einsum("mki,mkj->kij", first, second, precision=HIGH)

    real_part = outer(left[0], right[0]) + outer(left[1], right[1])
    imag_part = outer(left[1], right[0]) - outer(left[0], right[1])
    return jnp.stack([real_part, imag_part])


def shards(activations, cotangent, kept_modes, weight_in, bias_in, weight_out):
    field = activations[0]
    own_grad = cotangent[0]
    nblocks, width, rows, lon = field.shape
    channels = nblocks * width
    ndev = lax.axis_size("space")
    npipe = lax.axis_size("pipe")
    lat = rows * ndev
    share = KEEP_LON // ndev
    section = lax.axis_index("pipe")
    received = from_behind(own_grad, "pipe", -1)
    upstream = jnp.where(section == npipe - 1, own_grad, received)

    peaks = lax.all_gather(
        jnp.stack([largest(field), largest(own_grad)]), ("pipe", "space")
    ).reshape(npipe, ndev, 2)
    source = jnp.minimum(section + 1, npipe - 1)
    place = lax.axis_index("space")
    field_peaks = lax.dynamic_index_in_dim(peaks[:, :, 0], section, 0, False)
    grad_peaks = lax.dynamic_index_in_dim(peaks[:, :, 1], source, 0, False)

    lon_forward = jnp.asarray(lon_table(lon, ndev))
    lat_forward = jnp.asarray(lat_table(lat))

    def transform(values, peak, peaks_all):
        rows_first = jnp.swapaxes(values.reshape(channels, rows, lon), 0, 1)
        spectrum = jnp.einsum(
            "dpkn,lcn->dpklc", lon_forward, rows_first.astype(F32), precision=HIGH
        )
        sent = (spectrum * (1024.0 / peak)).astype(F16)
        got = lax.all_to_all(sent, "space", split_axis=0, concat_axis=0, tiled=True)
        table = lat_forward.reshape(2, 2 * KEEP_LAT, 2, ndev, rows)
        table = table * (peaks_all * (1.0 / 1024.0))[:, None]
        got = got.astype(F32)
        return jnp.einsum("qfpsl,spklc->qfkc", table, got, precision=HIGH)

    spec_field = transform(field, lax.dynamic_index_in_dim(field_peaks, place, 0, False), field_peaks)
    spec_grad = transform(upstream, lax.dynamic_index_in_dim(grad_peaks, place, 0, False), grad_peaks)

    signed = jnp.arange(2 * KEEP_LAT, dtype=jnp.int32) - KEEP_LAT
    wavenumber = place * share + jnp.arange(share, dtype=jnp.int32)
    mask = mode_mask(signed, wavenumber, kept_modes[0, 0], kept_modes[0, 1])
    modes = 2 * KEEP_LAT * share
    z = spec_field.reshape(2, modes, nblocks, width)
    g = (spec_grad * mask[:, :, None]).reshape(2, modes, nblocks, width)

    map_in, map_out = real_form(weight_in[0]), real_form(weight_out[0])
    before = jnp.einsum("pmkj,pkjqi->qmki", z, map_in, precision=HIGH) + bias_in[0][:, None]
    hidden, slope = gelu_pair(before)
    grad_hidden = jnp.einsum("qmki,pkjqi->pmkj", g, map_out, precision=HIGH)
    grad_before = grad_hidden * slope
    grad_modes = jnp.einsum("qmki,pkjqi->pmkj", grad_before, map_in, precision=HIGH)
    grads = (
        complex_outer(grad_before, z),
        jnp.sum(grad_before, axis=1),
        complex_outer(g, hidden),
        jnp.sum(g, axis=1),
    )

    peak = largest(grad_modes)
    back_peaks = lax.all_gather(peak, "space")
    grad_modes = grad_modes.reshape(2, 2 * KEEP_LAT, share, channels)
    lat_back = jnp.einsum(
        "qfpsl,qfkc->spklc",
        lat_forward.reshape(2, 2 * KEEP_LAT, 2, ndev, rows),
        grad_modes,
        precision=HIGH,
    )
    sent = (lat_back * (4000.0 / peak)).astype(F16)
    got = lax.all_to_all(sent, "space", split_axis=0, concat_axis=0, tiled=True).astype(F32)
    lon_back = lon_forward * (back_peaks * (1.0 / 4000.0))[:, None, None, None]
    inverse = jnp.einsum("dpkn,dpklc->lcn", lon_back, got, precision=HIGH)
    inverse = jnp.swapaxes(inverse, 0, 1).reshape(nblocks, width, rows, lon)
    grad_field = (upstream.astype(F32) + inverse).astype(jnp.bfloat16)

    sums = lax.psum(grads, "space")
    factor = 1.0 / math.sqrt(2 * KEEP_LAT * KEEP_LON)
    return (grad_field[None],) + tuple((s * factor)[None] for s in sums)


def solution(mesh):
    return jax.shard_map(
        shards,
        mesh=mesh,
        in_specs=(
            P("pipe", None, None, "space", None),
            P("pipe", None, None, "space", None),
            P("pipe", None),
            P("pipe", None, None, None, None),
            P("pipe", None, None, None),
            P("pipe", None, None, None, None),
        ),
        out_specs=(
            P("pipe", None, None, "space", None),
            P("pipe", None, None, None, None),
            P("pipe", None, None, None),
            P("pipe", None, None, None, None),
            P("pipe", None, None, None),
        ),
        check_vma=False,
    )
```

```python
import math

import jax
import jax.numpy as jnp
import numpy as np
from jax import lax
from jax.sharding import PartitionSpec as P

KEEP_LON = 128
KEEP_LAT = 64
HIGH = lax.Precision.HIGH
F32 = jnp.float32
F16 = jnp.float16


def from_behind(block, axis, distance):
    devices = range(lax.axis_size(axis))
    route = [(i - distance, i) for i in devices if i - distance in devices]
    return lax.ppermute(block, axis, route)


def lon_table(length, ndev):
    number = np.arange(KEEP_LON)[:, None] * np.arange(length)[None, :] % length
    angle = number * (2.0 * math.pi / length)
    table = np.stack([np.cos(angle), -np.sin(angle)]) / math.sqrt(length)
    table = table.reshape(2, ndev, KEEP_LON // ndev, length).transpose(1, 0, 2, 3)
    return table.astype(np.float32)


def lat_table(length):
    signed = np.arange(2 * KEEP_LAT) - KEEP_LAT
    angle = (signed[:, None] * np.arange(length)[None, :] % length) * (2.0 * math.pi / length)
    cos, sin = np.cos(angle) / math.sqrt(length), np.sin(angle) / math.sqrt(length)
    table = np.stack([np.stack([cos, sin], 1), np.stack([-sin, cos], 1)])
    return table.astype(np.float32)


def mode_mask(signed, wavenumber, keep_lon, keep_lat):
    lat_kept = (signed >= -keep_lat) & (signed < keep_lat)
    lon_kept = wavenumber < keep_lon
    factor = jnp.where(wavenumber == 0, 1.0, 2.0).astype(F32)
    return (lat_kept[:, None] & lon_kept[None, :]).astype(F32) * factor[None, :]


def real_form(weights):
    def diagonal(matrix):
        blocks, out, inner = matrix.shape
        eye = jnp.eye(blocks, dtype=F32)[:, None, :, None]
        return (jnp.swapaxes(matrix, 1, 2)[:, :, None, :] * eye).reshape(blocks * inner, blocks * out)

    re, im = diagonal(weights[0]), diagonal(weights[1])
    return jnp.stack([jnp.stack([re, im], 1), jnp.stack([-im, re], 1)])


def gelu_pair(values):
    inner = 0.7978845608 * (values + 0.044715 * values * values * values)
    tangent = jnp.tanh(inner)
    output = 0.5 * values * (1.0 + tangent)
    slope = 0.5 * (1.0 + tangent) + 0.5 * values * (1.0 - tangent * tangent) * 0.7978845608 * (
        1.0 + 3.0 * 0.044715 * values * values
    )
    return (output, slope)


def exponent(values):
    peak = jnp.maximum(jnp.max(jnp.abs(values.astype(F32))), 1e-30)
    return jnp.floor(jnp.log2(peak)) + 1.0


def packed(values, power, lanes):
    sent = (values * jnp.exp2(11.0 - power)).astype(F16)
    room = [(0, 0, 0)] * (sent.ndim - 1) + [(0, lanes, 0)]
    return lax.pad(sent, power.astype(F16), room)


def unpacked(got, channels):
    power = got[:, 0, 0, 0, channels].astype(F32)
    return got[..., :channels], jnp.exp2(power - 11.0)


def exchange(values):
    return lax.all_to_all(values, "space", split_axis=0, concat_axis=0, tiled=True)


def outer_gradient(left, right, nblocks, width):
    both = jnp.einsum("pfkc,qfkd->pcqd", left, right, precision=HIGH)
    sums = jnp.sum(left, axis=(1, 2))
    parts = []
    for re_or_im in range(2):
        for block in range(nblocks):
            here = slice(block * width, (block + 1) * width)
            if re_or_im == 0:
                value = both[0, here, 0, here] + both[1, here, 1, here]
            else:
                value = both[1, here, 0, here] - both[0, here, 1, here]
            parts.append(jnp.concatenate([value, sums[re_or_im, here][:, None]], axis=1))
    return jnp.concatenate(parts, axis=0)


def shards(activations, cotangent, kept_modes, weight_in, bias_in, weight_out):
    field = activations[0]
    own_grad = cotangent[0]
    nblocks, width, rows, lon = field.shape
    channels = nblocks * width
    lanes = -channels % 128
    ndev = lax.axis_size("space")
    lat = rows * ndev
    share = KEEP_LON // ndev
    last = lax.axis_index("pipe") == lax.axis_size("pipe") - 1
    place = lax.axis_index("space")

    lon_forward = jnp.asarray(lon_table(lon, ndev))
    lat_forward = jnp.asarray(lat_table(lat)).reshape(2, 2 * KEEP_LAT, 2, ndev, rows)

    def lon_spectrum(values):
        rows_first = jnp.swapaxes(values.reshape(channels, rows, lon), 0, 1)
        spectrum = jnp.einsum(
            "dpkn,lcn->dpklc", lon_forward, rows_first.astype(F32), precision=HIGH
        )
        return packed(spectrum, exponent(values), lanes)

    def lat_spectrum(sent):
        got, scale = unpacked(exchange(sent), channels)
        table = lat_forward * scale[:, None]
        return jnp.einsum("qfpsl,spklc->qfkc", table, got.astype(F32), precision=HIGH)

    own_sent = lon_spectrum(own_grad)
    other_sent = from_behind(own_sent, "pipe", -1)
    z = lat_spectrum(lon_spectrum(field))
    own_grad, other_sent = lax.optimization_barrier((own_grad, other_sent))
    received = from_behind(own_grad, "pipe", -1)
    spec_grad = lat_spectrum(jnp.where(last, own_sent, other_sent))

    signed = jnp.arange(2 * KEEP_LAT, dtype=jnp.int32) - KEEP_LAT
    wavenumber = place * share + jnp.arange(share, dtype=jnp.int32)
    mask = mode_mask(signed, wavenumber, kept_modes[0, 0], kept_modes[0, 1])
    g = spec_grad * mask[:, :, None]

    map_in, map_out = real_form(weight_in[0]), real_form(weight_out[0])
    bias = bias_in[0].reshape(2, 1, 1, channels)
    before = jnp.einsum("pfkc,pcqd->qfkd", z, map_in, precision=HIGH) + bias
    hidden, slope = gelu_pair(before)
    grad_hidden = jnp.einsum("qfkd,pcqd->pfkc", g, map_out, precision=HIGH)
    grad_before = grad_hidden * slope
    grad_modes = jnp.einsum("qfkd,pcqd->pfkc", grad_before, map_in, precision=HIGH)

    lat_back = jnp.einsum("qfpsl,qfkc->spklc", lat_forward, grad_modes, precision=HIGH)
    sent = packed(lat_back, exponent(grad_modes) + 4.0, lanes)
    got, scale = unpacked(exchange(sent), channels)
    lon_back = lon_forward * scale[:, None, None, None]
    inverse = jnp.einsum("dpkn,dpklc->lcn", lon_back, got.astype(F32), precision=HIGH)
    inverse = jnp.swapaxes(inverse, 0, 1).reshape(nblocks, width, rows, lon)
    upstream = jnp.where(last, own_grad, received)
    grad_field = (upstream.astype(F32) + inverse).astype(jnp.bfloat16)

    factor = 1.0 / math.sqrt(2 * KEEP_LAT * KEEP_LON)
    grads = jnp.concatenate(
        [
            outer_gradient(grad_before, z, nblocks, width),
            outer_gradient(g, hidden, nblocks, width),
        ],
        axis=0,
    )
    pieces = grads.reshape(ndev, -1, width + 1)
    piece = jnp.sum(exchange(pieces), axis=0) * factor
    sums = exchange(jnp.broadcast_to(piece[None], pieces.shape))
    sums = sums.reshape(2, 1, 2, nblocks, width, width + 1)
    return (
        grad_field[None],
        sums[0, ..., :width],
        sums[0, ..., width],
        sums[1, ..., :width],
        sums[1, ..., width],
    )


def solution(mesh):
    return jax.shard_map(
        shards,
        mesh=mesh,
        in_specs=(
            P("pipe", None, None, "space", None),
            P("pipe", None, None, "space", None),
            P("pipe", None),
            P("pipe", None, None, None, None),
            P("pipe", None, None, None),
            P("pipe", None, None, None, None),
        ),
        out_specs=(
            P("pipe", None, None, "space", None),
            P("pipe", None, None, None, None),
            P("pipe", None, None, None),
            P("pipe", None, None, None, None),
            P("pipe", None, None, None),
        ),
        check_vma=False,
    )
```

```python
import math

import jax
import jax.numpy as jnp
import numpy as np
from jax import lax
from jax.sharding import PartitionSpec as P

KEEP_LON = 128
KEEP_LAT = 64
HIGH = lax.Precision.HIGH
F32 = jnp.float32
F16 = jnp.float16


def from_behind(block, axis, distance):
    devices = range(lax.axis_size(axis))
    route = [(i - distance, i) for i in devices if i - distance in devices]
    return lax.ppermute(block, axis, route)


def lon_table(length, ndev):
    number = np.arange(KEEP_LON)[:, None] * np.arange(length)[None, :] % length
    angle = number * (2.0 * math.pi / length)
    table = np.stack([np.cos(angle), -np.sin(angle)]) / math.sqrt(length)
    table = table.reshape(2, ndev, KEEP_LON // ndev, length).transpose(1, 0, 2, 3)
    return table.astype(np.float32)


def lat_table(length):
    signed = np.arange(2 * KEEP_LAT) - KEEP_LAT
    angle = (signed[:, None] * np.arange(length)[None, :] % length) * (2.0 * math.pi / length)
    cos, sin = np.cos(angle) / math.sqrt(length), np.sin(angle) / math.sqrt(length)
    table = np.stack([np.stack([cos, sin], 1), np.stack([-sin, cos], 1)])
    return table.astype(np.float32)


def mode_mask(signed, wavenumber, keep_lon, keep_lat):
    lat_kept = (signed >= -keep_lat) & (signed < keep_lat)
    lon_kept = wavenumber < keep_lon
    factor = jnp.where(wavenumber == 0, 1.0, 2.0).astype(F32)
    return (lat_kept[:, None] & lon_kept[None, :]).astype(F32) * factor[None, :]


def real_form(weights):
    def diagonal(matrix):
        blocks, out, inner = matrix.shape
        eye = jnp.eye(blocks, dtype=F32)[:, None, :, None]
        return (jnp.swapaxes(matrix, 1, 2)[:, :, None, :] * eye).reshape(blocks * inner, blocks * out)

    re, im = diagonal(weights[0]), diagonal(weights[1])
    return jnp.stack([jnp.stack([re, im], 1), jnp.stack([-im, re], 1)])


def gelu_pair(values):
    inner = 0.7978845608 * (values + 0.044715 * values * values * values)
    tangent = jnp.tanh(inner)
    output = 0.5 * values * (1.0 + tangent)
    slope = 0.5 * (1.0 + tangent) + 0.5 * values * (1.0 - tangent * tangent) * 0.7978845608 * (
        1.0 + 3.0 * 0.044715 * values * values
    )
    return (output, slope)


def exponent(values):
    peak = jnp.maximum(jnp.max(jnp.abs(values.astype(F32))), 1e-30)
    return jnp.floor(jnp.log2(peak)) + 1.0


def packed(values, power, lanes):
    sent = (values * jnp.exp2(11.0 - power)).astype(F16)
    room = [(0, 0, 0)] * (sent.ndim - 1) + [(0, lanes, 0)]
    return lax.pad(sent, power.astype(F16), room)


def unpacked(got, channels):
    power = got[:, 0, 0, 0, channels].astype(F32)
    return got[..., :channels], jnp.exp2(power - 11.0)


def exchange(values):
    return lax.all_to_all(values, "space", split_axis=0, concat_axis=0, tiled=True)


def outer_gradient(left, right, nblocks, width):
    both = jnp.einsum("pfkc,qfkd->pcqd", left, right, precision=HIGH)
    sums = jnp.sum(left, axis=(1, 2))
    parts = []
    for re_or_im in range(2):
        for block in range(nblocks):
            here = slice(block * width, (block + 1) * width)
            if re_or_im == 0:
                value = both[0, here, 0, here] + both[1, here, 1, here]
            else:
                value = both[1, here, 0, here] - both[0, here, 1, here]
            parts.append(jnp.concatenate([value, sums[re_or_im, here][:, None]], axis=1))
    return jnp.concatenate(parts, axis=0)


def shards(activations, cotangent, kept_modes, weight_in, bias_in, weight_out):
    field = activations[0]
    own_grad = cotangent[0]
    nblocks, width, rows, lon = field.shape
    channels = nblocks * width
    lanes = -channels % 128
    ndev = lax.axis_size("space")
    lat = rows * ndev
    share = KEEP_LON // ndev
    last = lax.axis_index("pipe") == lax.axis_size("pipe") - 1
    place = lax.axis_index("space")

    lon_forward = jnp.asarray(lon_table(lon, ndev))
    lat_forward = jnp.asarray(lat_table(lat)).reshape(2, 2 * KEEP_LAT, 2, ndev, rows)

    def lon_spectrum(values):
        rows_first = jnp.swapaxes(values.reshape(channels, rows, lon), 0, 1)
        spectrum = jnp.einsum(
            "dpkn,lcn->dpklc", lon_forward, rows_first.astype(F32), precision=HIGH
        )
        return packed(spectrum, exponent(values), lanes)

    def lat_spectrum(sent):
        got, scale = unpacked(exchange(sent), channels)
        table = lat_forward * scale[:, None]
        return jnp.einsum("qfpsl,spklc->qfkc", table, got.astype(F32), precision=HIGH)

    own_sent = lon_spectrum(own_grad)
    other_sent = from_behind(own_sent, "pipe", -1)
    z = lat_spectrum(lon_spectrum(field))
    own_grad, other_sent = lax.optimization_barrier((own_grad, other_sent))
    received = from_behind(own_grad, "pipe", -1)
    spec_grad = lat_spectrum(jnp.where(last, own_sent, other_sent))

    signed = jnp.arange(2 * KEEP_LAT, dtype=jnp.int32) - KEEP_LAT
    wavenumber = place * share + jnp.arange(share, dtype=jnp.int32)
    mask = mode_mask(signed, wavenumber, kept_modes[0, 0], kept_modes[0, 1])
    g = spec_grad * mask[:, :, None]

    map_in, map_out = real_form(weight_in[0]), real_form(weight_out[0])
    bias = bias_in[0].reshape(2, 1, 1, channels)
    before = jnp.einsum("pfkc,pcqd->qfkd", z, map_in, precision=HIGH) + bias
    hidden, slope = gelu_pair(before)
    grad_hidden = jnp.einsum("qfkd,pcqd->pfkc", g, map_out, precision=HIGH)
    grad_before = grad_hidden * slope
    grad_modes = jnp.einsum("qfkd,pcqd->pfkc", grad_before, map_in, precision=HIGH)

    lat_back = jnp.einsum("qfpsl,qfkc->spklc", lat_forward, grad_modes, precision=HIGH)
    sent = packed(lat_back, exponent(grad_modes) + 4.0, lanes)
    _, received, grad_before, z, g, hidden = lax.optimization_barrier(
        (sent, received, grad_before, z, g, hidden)
    )
    got, scale = unpacked(exchange(sent), channels)
    lon_back = lon_forward * scale[:, None, None, None]
    inverse = jnp.einsum("dpkn,dpklc->lcn", lon_back, got.astype(F32), precision=HIGH)
    inverse = jnp.swapaxes(inverse, 0, 1).reshape(nblocks, width, rows, lon)
    upstream = jnp.where(last, own_grad, received)
    grad_field = (upstream.astype(F32) + inverse).astype(jnp.bfloat16)

    factor = 1.0 / math.sqrt(2 * KEEP_LAT * KEEP_LON)
    grads = jnp.concatenate(
        [
            outer_gradient(grad_before, z, nblocks, width),
            outer_gradient(g, hidden, nblocks, width),
        ],
        axis=0,
    )
    pieces = grads.reshape(ndev, -1, width + 1)
    piece = jnp.sum(exchange(pieces), axis=0) * factor
    sums = exchange(jnp.broadcast_to(piece[None], pieces.shape))
    sums = sums.reshape(2, 1, 2, nblocks, width, width + 1)
    return (
        grad_field[None],
        sums[0, ..., :width],
        sums[0, ..., width],
        sums[1, ..., :width],
        sums[1, ..., width],
    )


def solution(mesh):
    return jax.shard_map(
        shards,
        mesh=mesh,
        in_specs=(
            P("pipe", None, None, "space", None),
            P("pipe", None, None, "space", None),
            P("pipe", None),
            P("pipe", None, None, None, None),
            P("pipe", None, None, None),
            P("pipe", None, None, None, None),
        ),
        out_specs=(
            P("pipe", None, None, "space", None),
            P("pipe", None, None, None, None),
            P("pipe", None, None, None),
            P("pipe", None, None, None, None),
            P("pipe", None, None, None),
        ),
        check_vma=False,
    )
```

```python
import math

import jax
import jax.numpy as jnp
import numpy as np
from jax import lax
from jax.sharding import PartitionSpec as P

KEEP_LON = 128
KEEP_LAT = 64
HIGH = lax.Precision.HIGH
F32 = jnp.float32
F16 = jnp.float16


def from_behind(block, axis, distance):
    devices = range(lax.axis_size(axis))
    route = [(i - distance, i) for i in devices if i - distance in devices]
    return lax.ppermute(block, axis, route)


def lon_table(length, ndev):
    number = np.arange(KEEP_LON)[:, None] * np.arange(length)[None, :] % length
    angle = number * (2.0 * math.pi / length)
    table = np.stack([np.cos(angle), -np.sin(angle)]) / math.sqrt(length)
    table = table.reshape(2, ndev, KEEP_LON // ndev, length).transpose(1, 0, 2, 3)
    return table.astype(np.float32)


def lat_table(length):
    signed = np.arange(2 * KEEP_LAT) - KEEP_LAT
    angle = (signed[:, None] * np.arange(length)[None, :] % length) * (2.0 * math.pi / length)
    cos, sin = np.cos(angle) / math.sqrt(length), np.sin(angle) / math.sqrt(length)
    table = np.stack([np.stack([cos, sin], 1), np.stack([-sin, cos], 1)])
    return table.astype(np.float32)


def mode_mask(signed, wavenumber, keep_lon, keep_lat):
    lat_kept = (signed >= -keep_lat) & (signed < keep_lat)
    lon_kept = wavenumber < keep_lon
    factor = jnp.where(wavenumber == 0, 1.0, 2.0).astype(F32)
    return (lat_kept[:, None] & lon_kept[None, :]).astype(F32) * factor[None, :]


def real_form(weights):
    def diagonal(matrix):
        blocks, out, inner = matrix.shape
        eye = jnp.eye(blocks, dtype=F32)[:, None, :, None]
        return (jnp.swapaxes(matrix, 1, 2)[:, :, None, :] * eye).reshape(blocks * inner, blocks * out)

    re, im = diagonal(weights[0]), diagonal(weights[1])
    return jnp.stack([jnp.stack([re, im], 1), jnp.stack([-im, re], 1)])


def gelu_pair(values):
    inner = 0.7978845608 * (values + 0.044715 * values * values * values)
    tangent = jnp.tanh(inner)
    output = 0.5 * values * (1.0 + tangent)
    slope = 0.5 * (1.0 + tangent) + 0.5 * values * (1.0 - tangent * tangent) * 0.7978845608 * (
        1.0 + 3.0 * 0.044715 * values * values
    )
    return (output, slope)


def exponent(values):
    peak = jnp.maximum(jnp.max(jnp.abs(values.astype(F32))), 1e-30)
    return jnp.floor(jnp.log2(peak)) + 1.0


def packed(values, power, lanes):
    sent = (values * jnp.exp2(11.0 - power)).astype(F16)
    room = [(0, 0, 0)] * (sent.ndim - 1) + [(0, lanes, 0)]
    return lax.pad(sent, power.astype(F16), room)


def unpacked(got, channels):
    power = got[:, 0, 0, 0, channels].astype(F32)
    return got[..., :channels], jnp.exp2(power - 11.0)


def exchange(values):
    return lax.all_to_all(values, "space", split_axis=0, concat_axis=0, tiled=True)


def outer_gradient(left, right, nblocks, width):
    both = jnp.einsum("pfkc,qfkd->pcqd", left, right, precision=HIGH)
    sums = jnp.sum(left, axis=(1, 2))
    parts = []
    for re_or_im in range(2):
        for block in range(nblocks):
            here = slice(block * width, (block + 1) * width)
            if re_or_im == 0:
                value = both[0, here, 0, here] + both[1, here, 1, here]
            else:
                value = both[1, here, 0, here] - both[0, here, 1, here]
            parts.append(jnp.concatenate([value, sums[re_or_im, here][:, None]], axis=1))
    return jnp.concatenate(parts, axis=0)


def shards(activations, cotangent, kept_modes, weight_in, bias_in, weight_out):
    field = activations[0]
    own_grad = cotangent[0]
    nblocks, width, rows, lon = field.shape
    channels = nblocks * width
    lanes = -channels % 128
    ndev = lax.axis_size("space")
    lat = rows * ndev
    share = KEEP_LON // ndev
    last = lax.axis_index("pipe") == lax.axis_size("pipe") - 1
    place = lax.axis_index("space")

    lon_forward = jnp.asarray(lon_table(lon, ndev))
    lat_forward = jnp.asarray(lat_table(lat)).reshape(2, 2 * KEEP_LAT, 2, ndev, rows)

    def lon_spectrum(values):
        rows_first = jnp.swapaxes(values.reshape(channels, rows, lon), 0, 1)
        spectrum = jnp.einsum(
            "dpkn,lcn->dpklc", lon_forward, rows_first.astype(F32), precision=HIGH
        )
        return packed(spectrum, exponent(values), lanes)

    def lat_spectrum(sent):
        got, scale = unpacked(exchange(sent), channels)
        table = lat_forward * scale[:, None]
        return jnp.einsum("qfpsl,spklc->qfkc", table, got.astype(F32), precision=HIGH)

    own_sent = lon_spectrum(own_grad)
    other_sent = from_behind(own_sent, "pipe", -1)
    z = lat_spectrum(lon_spectrum(field))
    own_grad, other_sent = lax.optimization_barrier((own_grad, other_sent))
    received = from_behind(own_grad, "pipe", -1)
    spec_grad = lat_spectrum(jnp.where(last, own_sent, other_sent))

    signed = jnp.arange(2 * KEEP_LAT, dtype=jnp.int32) - KEEP_LAT
    wavenumber = place * share + jnp.arange(share, dtype=jnp.int32)
    mask = mode_mask(signed, wavenumber, kept_modes[0, 0], kept_modes[0, 1])
    g = spec_grad * mask[:, :, None]

    map_in, map_out = real_form(weight_in[0]), real_form(weight_out[0])
    bias = bias_in[0].reshape(2, 1, 1, channels)
    before = jnp.einsum("pfkc,pcqd->qfkd", z, map_in, precision=HIGH) + bias
    hidden, slope = gelu_pair(before)
    grad_hidden = jnp.einsum("qfkd,pcqd->pfkc", g, map_out, precision=HIGH)
    grad_before = grad_hidden * slope
    grad_modes = jnp.einsum("qfkd,pcqd->pfkc", grad_before, map_in, precision=HIGH)

    lat_back = jnp.einsum("qfpsl,qfkc->spklc", lat_forward, grad_modes, precision=HIGH)
    sent = packed(lat_back, exponent(grad_modes) + 4.0, lanes)
    _, received, grad_before, z, g, hidden = lax.optimization_barrier(
        (sent, received, grad_before, z, g, hidden)
    )
    factor = 1.0 / math.sqrt(2 * KEEP_LAT * KEEP_LON)
    grads = jnp.concatenate(
        [
            outer_gradient(grad_before, z, nblocks, width),
            outer_gradient(g, hidden, nblocks, width),
        ],
        axis=0,
    )
    pieces = grads.reshape(ndev, -1, width + 1)
    piece = jnp.sum(exchange(pieces), axis=0) * factor
    got, piece = lax.optimization_barrier((exchange(sent), piece))
    got, scale = unpacked(got, channels)
    lon_back = lon_forward * scale[:, None, None, None]
    inverse = jnp.einsum("dpkn,dpklc->lcn", lon_back, got.astype(F32), precision=HIGH)
    inverse = jnp.swapaxes(inverse, 0, 1).reshape(nblocks, width, rows, lon)
    upstream = jnp.where(last, own_grad, received)
    grad_field = (upstream.astype(F32) + inverse).astype(jnp.bfloat16)

    sums = exchange(jnp.broadcast_to(piece[None], pieces.shape))
    sums = sums.reshape(2, 1, 2, nblocks, width, width + 1)
    return (
        grad_field[None],
        sums[0, ..., :width],
        sums[0, ..., width],
        sums[1, ..., :width],
        sums[1, ..., width],
    )


def solution(mesh):
    return jax.shard_map(
        shards,
        mesh=mesh,
        in_specs=(
            P("pipe", None, None, "space", None),
            P("pipe", None, None, "space", None),
            P("pipe", None),
            P("pipe", None, None, None, None),
            P("pipe", None, None, None),
            P("pipe", None, None, None, None),
        ),
        out_specs=(
            P("pipe", None, None, "space", None),
            P("pipe", None, None, None, None),
            P("pipe", None, None, None),
            P("pipe", None, None, None, None),
            P("pipe", None, None, None),
        ),
        check_vma=False,
    )
```
